32 devices in a mesh: grp: 2 (over x), row: 16 (over z, y, core).
Axes of the slice: x: 2, y: 2, z: 4, core: 2. Of those that a mesh axis runs over, the one named last changes fastest.
Arguments:
- populations: float32 [32768, 512], P(('grp', 'row')), parts along dimension 0
- rate_blocks: float32 [256, 6, 2, 128, 128], P(('grp', 'row')), parts along dimension 0
- columns: int32 [256, 6, 2], P(('grp', 'row')), parts along dimension 0, may hold values from 0 to 7
- counts: int32 [256, 6], P(('grp', 'row')), parts along dimension 0, may hold values from 0 to 2, as said below
- owners: int32 [6], replicated, may hold values from 0 to 15, as said below
Outputs:
- krylov_basis: float32 [32768, 512], P(('grp', 'row')), parts along dimension 0
- chain_scale: float32 [1024], P('grp'), parts along dimension 0
The draws below stay inside these ranges and needn't reach their ends.
There are 2 independent parts, one for each index of `grp`. The reference program is written for one: setup_inputs(seed, part) draws one part's arguments, and reference() takes and returns one part's arrays. A program takes and returns all parts, laid end to end along the dimension named above; an argument that names none is the same for every part. Nothing has to cross between parts.
Inputs may be any that keep to these rules, and one draw needn't show every extreme that they name: `owners`: distinct devices of the row axis. `counts`: in every panel some block row has 2 live slots.
All inputs are finite; a program needn't handle non-finite values.
Results may differ from the reference program's by a relative error of at most 0.0001.
Values sent between devices are 32-bit elements; how exact they have to be, the bound alone decides.
A program may use at most 128 MiB of HBM per device.

```python
import jax
import jax.numpy as jnp
from jax import lax

BLK = 128
BR_DEV = 8
CHAINS = 512
PANELS = 6
SLOTS = 2
NB = 128
LEVELS = 16384
N_ROW = 16


def draw_populations(key, part):
    key = jax.random.fold_in(key, 11)
    key_a, key_b = jax.random.split(key, 2)
    chain_level = 10.0 ** jax.random.uniform(key_b, (CHAINS,), jnp.float32)
    values = jax.random.normal(key_a, (LEVELS, CHAINS), jnp.float32)
    return values * (0.3 * chain_level)[None, :]


def draw_rate_blocks(key, part):
    key = jax.random.fold_in(key, 12)
    key_a, key_b = jax.random.split(key)
    shape_all = (NB, PANELS, SLOTS, BLK, BLK)
    values = jax.random.normal(key_a, shape_all, jnp.float32)
    block_pos = jnp.arange(NB, dtype=jnp.float32) / NB
    row_level = 0.3 * 10.0 ** block_pos
    rough = jax.random.uniform(key_b, (NB, 1, 1, BLK, 1), jnp.float32, 0.5, 2.0)
    return values * rough * row_level[:, None, None, None, None] * (BLK * PANELS) ** (-0.5)


def draw_columns(key, part):
    key = jax.random.fold_in(key, 13)
    return jax.random.randint(key, (NB, PANELS, SLOTS), 0, BR_DEV, jnp.int32)


def draw_counts(key, part):
    key = jax.random.fold_in(key, 14)
    key_a, key_b, key_c = jax.random.split(key, 3)
    device_level = jax.random.randint(key_a, (NB // BR_DEV,), 1, SLOTS + 1, jnp.int32)
    row_level = jnp.repeat(device_level, BR_DEV)
    lowered = jax.random.randint(key_b, (NB, PANELS), 0, 2, jnp.int32)
    values = jnp.maximum(row_level[:, None] - lowered, 0)
    full_row = jax.random.randint(key_c, (), 0, NB, jnp.int32)
    return values.at[full_row, :].set(SLOTS)


def draw_owners(key, part):
    key = jax.random.fold_in(key, 15)
    return jax.random.permutation(key, N_ROW)[:PANELS].astype(jnp.int32)


def setup_inputs(seed: int = 0, part: int = 0) -> dict:
    splits = jax.random.split(jax.random.key(seed), 6)
    own_keys = jax.random.split(jax.random.fold_in(splits[5], part), 6)
    populations = draw_populations(jax.random.fold_in(jax.random.fold_in(splits[5], part), 71), part)
    rate_blocks = draw_rate_blocks(jax.random.fold_in(jax.random.fold_in(splits[5], part), 71), part)
    columns = draw_columns(jax.random.fold_in(jax.random.fold_in(splits[5], part), 71), part)
    counts = draw_counts(jax.random.fold_in(jax.random.fold_in(splits[5], part), 71), part)
    owners = draw_owners(jax.random.fold_in(splits[5], 71), part)
    return dict(populations=populations, rate_blocks=rate_blocks, columns=columns, counts=counts, owners=owners)


def reference(populations, rate_blocks, columns, counts, owners):
    running = jnp.zeros((NB, BLK, CHAINS), jnp.float32)
    for k in range(PANELS):
        start_row = (owners[k] * (BR_DEV * BLK)).astype(jnp.int32)
        panel_rows = lax.dynamic_slice_in_dim(populations, start_row, BR_DEV * BLK, 0)
        panel_blocks = panel_rows.reshape(BR_DEV, BLK, CHAINS)
        for s in range(SLOTS):
            picked = panel_blocks[columns[:, k, s]]
            live_mask = (s < counts[:, k]).astype(jnp.float32)
            weight = rate_blocks[:, k, s] * live_mask[:, None, None]
            running = running + jnp.einsum('rij,rjc->ric', weight, picked, precision=lax.Precision.HIGHEST)
    product = running.reshape(NB * BLK, CHAINS)
    chain_scale = jnp.sqrt(lax.optimization_barrier(jnp.sum(product * product, axis=0)) / (NB * BLK) + 1e-06)
    return (product / chain_scale, chain_scale)
```

```python
import functools

import jax
import jax.numpy as jnp
from jax import lax
from jax.experimental import pallas as pl
from jax.experimental.pallas import tpu as pltpu
from jax.sharding import PartitionSpec as P

CHUNKS = 4
SKEW = 2
LAG_Y = 2
LAG_C = 1
MESH = pl.DeviceIdType.MESH


def grid_of(devices):
    pairs = devices // 2
    nb = 1
    while (nb * 2) * (nb * 2) <= pairs:
        nb *= 2
    return pairs // nb, nb


def split(x):
    high = x.astype(jnp.bfloat16)
    low = (x - high.astype(jnp.float32)).astype(jnp.bfloat16)
    return high, low


def kernel(na, nb, chunks, panels, pop, rates, columns, counts, owners, product, squares,
           weight_f32, weights, y_in, core_in, plane, up, down, full, high, low, acc,
           sum_mine, sum_y, sum_core, sum_a, weight_sem,
           yp_s, yp_r, cp_s, cp_r, up_s, up_r, dn_s, dn_r, yq_s, yq_r, cq_s, cq_r,
           sy_s, sy_r, sc_s, sc_r, sa_s, sa_r):
    me = lax.axis_index("row")
    core = lax.rem(me, 2)
    b = lax.rem(me // 2, nb)
    a = me // (2 * nb)
    other = 1 - core
    units = chunks * panels
    width = pop.shape[3] // chunks
    block_rows, block_size = product.shape[0], product.shape[1]

    def at(a_, b_, core_):
        return {"row": (a_ * nb + b_) * 2 + core_}

    def b_plus(d):
        return lax.rem(b + d, nb)

    def b_minus(d):
        return lax.rem(b + nb - d, nb)

    def remote(src, dst, send, recv, where):
        return pltpu.make_async_remote_copy(
            src_ref=src, dst_ref=dst, send_sem=send, recv_sem=recv,
            device_id=where, device_id_type=MESH)

    load_weights = pltpu.make_async_copy(rates, weight_f32, weight_sem)
    load_weights.start()

    barrier = pltpu.get_barrier_semaphore()
    pl.semaphore_signal(barrier, inc=1, device_id=at(a, b, other), device_id_type=MESH)
    for d in range(1, nb):
        pl.semaphore_signal(barrier, inc=1, device_id=at(a, b_plus(d), core), device_id_type=MESH)
    for d in range(1, na):
        pl.semaphore_signal(barrier, inc=1, device_id=at(lax.rem(a + d, na), b, core),
                            device_id_type=MESH)
    pl.semaphore_wait(barrier, 1 + (nb - 1) + (na - 1))

    def y_pre(c, d):
        return remote(pop.at[:, b_plus(d), :, pl.ds(c * width, width)], y_in.at[c, d - 1],
                      yp_s.at[c, d - 1], yp_r.at[c, d - 1], at(a, b_plus(d), core))

    def core_pre(c, e):
        if e == 0:
            src = pop.at[other, b, :, pl.ds(c * width, width)]
        else:
            src = y_in.at[c, e - 1, other]
        return remote(src, core_in.at[c, e], cp_s.at[c, e], cp_r.at[c, e], at(a, b, other))

    def start_y(c):
        for d in range(1, nb):
            y_pre(c, d).start()

    def turn(c):
        for d in range(1, nb):
            y_pre(c, d).wait_recv()
        for e in range(nb):
            core_pre(c, e).start()

    def assemble(c):
        for e in range(nb):
            core_pre(c, e).wait_recv()
        plane[c, b * 2 + core] = pop[core, b, :, c * width:(c + 1) * width]
        plane[c, b * 2 + other] = core_in[c, 0]
        for d in range(1, nb):
            plane[c, b_minus(d) * 2 + core] = y_in[c, d - 1, core]
            plane[c, b_minus(d) * 2 + other] = core_in[c, d]

    start_y(0)
    acc[...] = jnp.zeros_like(acc)
    turn(0)
    if chunks > 1:
        start_y(1)
    assemble(0)
    load_weights.wait()

    def up_copy(u):
        return remote(up.at[u], up.at[u], up_s.at[u], up_r.at[u], at(a + 1, b, core))

    def down_copy(u):
        return remote(down.at[u], down.at[u], dn_s.at[u], dn_r.at[u], at(a - 1, b, core))

    def y_post(u, d):
        return remote(full.at[u, core, b], full.at[u, core, b],
                      yq_s.at[u, d - 1], yq_r.at[u, d - 1], at(a, b_plus(d), core))

    def y_landed(u, d):
        here = full.at[u, core, b_minus(d)]
        return remote(here, here, yq_s.at[u, d - 1], yq_r.at[u, d - 1], at(a, b_minus(d), core))

    def core_post(u):
        return remote(full.at[u, core], full.at[u, core], cq_s.at[u], cq_r.at[u], at(a, b, other))

    def core_landed(u):
        return remote(full.at[u, other], full.at[u, other], cq_s.at[u], cq_r.at[u],
                      at(a, b, other))

    def flow(u, buffer, copy, first, last):
        k = lax.rem(u, panels)
        owner = owners[k]

        @pl.when(first)
        def _():
            buffer[u] = plane[u // panels, lax.rem(owner, 2 * nb)]

        @pl.when(jnp.logical_not(first))
        def _():
            copy(u).wait_recv()
            picked = plane[u // panels, lax.rem(owner, 2 * nb)]
            buffer[u] = jnp.where(owner // (2 * nb) == a, picked, buffer[u])

        @pl.when(jnp.logical_not(last))
        def _():
            copy(u).start()

    def prepare(k):
        def body(r, carry):
            for s in range(2):
                live = (s < counts[r, k]).astype(jnp.float32)
                hi, lo = split(weight_f32[r, k, s] * live)
                weights[k, r, 0:block_size, s * block_size:(s + 1) * block_size] = hi
                weights[k, r, block_size:2 * block_size,
                        s * block_size:(s + 1) * block_size] = lo
            return carry

        lax.fori_loop(0, block_rows, body, 0)

    def multiply(u):
        k = lax.rem(u, panels)
        c = u // panels

        @pl.when(u < panels)
        def _():
            prepare(k)

        hi, lo = split(full[u].reshape(block_rows, block_size, width))
        high[...] = hi
        low[...] = lo

        def body(r, carry):
            first, second = columns[r, k, 0], columns[r, k, 1]
            w = weights[k, r]
            p_hi = jnp.concatenate([high[first], high[second]], axis=0)
            p_lo = jnp.concatenate([low[first], low[second]], axis=0)
            both = jnp.dot(w, p_hi, preferred_element_type=jnp.float32)
            cross = jnp.dot(w[0:block_size], p_lo, preferred_element_type=jnp.float32)
            acc[c, r] += both[0:block_size] + (both[block_size:2 * block_size] + cross)
            return carry

        lax.fori_loop(0, block_rows, body, 0, unroll=True)

    def step(t, carry):
        for c in range(1, chunks):
            @pl.when(t == max(c * panels - 4, 0))
            def _():
                turn(c)
                if c + 1 < chunks:
                    start_y(c + 1)

            @pl.when(t == max(c * panels - 2, 0))
            def _():
                assemble(c)

        lag_up, lag_down = SKEW * a, SKEW * (na - 1 - a)
        u_up, u_down = t - lag_up, t - lag_down
        u_y = t - jnp.maximum(lag_up, lag_down)
        u_c = u_y - LAG_Y
        u_m = u_c - LAG_C

        @pl.when((u_up >= 0) & (u_up < units))
        def _():
            flow(u_up, up, up_copy, a == 0, a == na - 1)

        @pl.when((u_down >= 0) & (u_down < units))
        def _():
            flow(u_down, down, down_copy, a == na - 1, a == 0)

        @pl.when((u_y >= 0) & (u_y < units))
        def _():
            owner_a = owners[lax.rem(u_y, panels)] // (2 * nb)
            full[u_y, core, b] = jnp.where(owner_a <= a, up[u_y], down[u_y])
            for d in range(1, nb):
                y_post(u_y, d).start()

        @pl.when((u_c >= 0) & (u_c < units))
        def _():
            for d in range(1, nb):
                y_landed(u_c, d).wait_recv()
            core_post(u_c).start()

        @pl.when((u_m >= 0) & (u_m < units))
        def _():
            core_landed(u_m).wait_recv()
            multiply(u_m)

        return carry

    lax.fori_loop(0, units + SKEW * (na - 1) + LAG_Y + LAG_C, step, 0)

    for c in range(chunks):
        x = acc[c].reshape(block_rows * block_size // 8, 8, width)
        sum_mine[0, :, c * width:(c + 1) * width] = jnp.sum(x * x, axis=0)

    def sum_c():
        return remote(sum_mine.at[0], sum_core, sc_s, sc_r, at(a, b, other))

    def sum_b(d):
        return remote(sum_mine.at[1], sum_y.at[d - 1], sy_s.at[d - 1], sy_r.at[d - 1],
                      at(a, b_plus(d), core))

    def sum_over_a(d):
        return remote(sum_mine.at[2], sum_a.at[d - 1], sa_s.at[d - 1], sa_r.at[d - 1],
                      at(lax.rem(a + d, na), b, core))

    sum_c().start()
    for c in range(chunks):
        product[:, :, c * width:(c + 1) * width] = acc[c]
    sum_c().wait_recv()
    sum_mine[1] = sum_mine[0] + sum_core[...]
    for d in range(1, nb):
        sum_b(d).start()
    total = sum_mine[1]
    for d in range(1, nb):
        sum_b(d).wait_recv()
        total = total + sum_y[d - 1]
    sum_mine[2] = total
    for d in range(1, na):
        sum_over_a(d).start()
    for d in range(1, na):
        sum_over_a(d).wait_recv()
        total = total + sum_a[d - 1]
    squares[...] = total

    sum_c().wait_send()
    for d in range(1, nb):
        sum_b(d).wait_send()
    for d in range(1, na):
        sum_over_a(d).wait_send()
    for c in range(chunks):
        for d in range(1, nb):
            y_pre(c, d).wait_send()
        for e in range(nb):
            core_pre(c, e).wait_send()

    def drain(u, carry):
        @pl.when(a < na - 1)
        def _():
            up_copy(u).wait_send()

        @pl.when(a > 0)
        def _():
            down_copy(u).wait_send()

        for d in range(1, nb):
            y_post(u, d).wait_send()
        core_post(u).wait_send()
        return carry

    lax.fori_loop(0, units, drain, 0)


def on_device(devices, populations, rate_blocks, columns, counts, owners):
    block_rows, panels, slots, block_size, _ = rate_blocks.shape
    rows, chains = populations.shape
    na, nb = grid_of(devices)
    chunks = CHUNKS
    units = chunks * panels
    width = chains // chunks
    lane_rows = rows // (2 * nb)
    f32, bf16 = jnp.float32, jnp.bfloat16
    vmem = pl.BlockSpec(memory_space=pltpu.VMEM)
    smem = pl.BlockSpec(memory_space=pltpu.SMEM)
    dma = pltpu.SemaphoreType.DMA
    product, squares = pl.pallas_call(
        functools.partial(kernel, na, nb, chunks, panels),
        out_shape=(jax.ShapeDtypeStruct((block_rows, block_size, chains), f32),
                   jax.ShapeDtypeStruct((8, chains), f32)),
        in_specs=[vmem, pl.BlockSpec(memory_space=pl.ANY), smem, smem, smem],
        out_specs=(vmem, vmem),
        scratch_shapes=[
            pltpu.VMEM((block_rows, panels, slots, block_size, block_size), f32),
            pltpu.VMEM((panels, block_rows, 2 * block_size, slots * block_size), bf16),
            pltpu.VMEM((chunks, nb - 1, 2, lane_rows, width), f32),
            pltpu.VMEM((chunks, nb, lane_rows, width), f32),
            pltpu.VMEM((chunks, 2 * nb, lane_rows, width), f32),
            pltpu.VMEM((units, lane_rows, width), f32),
            pltpu.VMEM((units, lane_rows, width), f32),
            pltpu.VMEM((units, 2, nb, lane_rows, width), f32),
            pltpu.VMEM((block_rows, block_size, width), bf16),
            pltpu.VMEM((block_rows, block_size, width), bf16),
            pltpu.VMEM((chunks, block_rows, block_size, width), f32),
            pltpu.VMEM((3, 8, chains), f32),
            pltpu.VMEM((nb - 1, 8, chains), f32),
            pltpu.VMEM((8, chains), f32),
            pltpu.VMEM((na - 1, 8, chains), f32),
            dma,
            dma((chunks, nb - 1)), dma((chunks, nb - 1)),
            dma((chunks, nb)), dma((chunks, nb)),
            dma((units,)), dma((units,)),
            dma((units,)), dma((units,)),
            dma((units, nb - 1)), dma((units, nb - 1)),
            dma((units,)), dma((units,)),
            dma((nb - 1,)), dma((nb - 1,)),
            dma, dma,
            dma((na - 1,)), dma((na - 1,)),
        ],
        compiler_params=pltpu.CompilerParams(
            collective_id=0, has_side_effects=True, vmem_limit_bytes=56 * 1024 * 1024),
        cost_estimate=pl.CostEstimate(
            flops=6 * block_rows * panels * slots * block_size * block_size * chains,
            bytes_accessed=4 * (rate_blocks.size + 2 * populations.size), transcendentals=0),
    )(populations.reshape(2, nb, lane_rows, chains), rate_blocks, columns, counts, owners)
    chain_scale = jnp.sqrt(jnp.sum(squares, axis=0) / (rows * devices) + 1e-06)
    return product.reshape(rows, chains) / chain_scale, chain_scale


def solution(mesh):
    in_specs = (
        P(("grp", "row"), None),
        P(("grp", "row"), None, None, None, None),
        P(("grp", "row"), None, None),
        P(("grp", "row"), None),
        P(),
    )
    out_specs = (P(("grp", "row"), None), P("grp"))
    return jax.shard_map(
        functools.partial(on_device, mesh.shape["row"]),
        mesh=mesh, in_specs=in_specs, out_specs=out_specs, check_vma=False)
```

```python
import functools

import jax
import jax.numpy as jnp
from jax import lax
from jax.experimental import pallas as pl
from jax.experimental.pallas import tpu as pltpu
from jax.sharding import PartitionSpec as P

CHUNKS = 4
PIECES = 1
THROTTLE = 0
SKEW = 2
LAG_Y = 2
LAG_C = 2
MESH = pl.DeviceIdType.MESH


def grid_of(devices):
    pairs = devices // 2
    nb = 1
    while (nb * 2) * (nb * 2) <= pairs:
        nb *= 2
    return pairs // nb, nb


def split(x):
    high = x.astype(jnp.bfloat16)
    low = (x - high.astype(jnp.float32)).astype(jnp.bfloat16)
    return high, low


def kernel(na, nb, chunks, pieces, panels, pop, rates, columns, counts, owners, product, squares,
           weight_f32, weights, y_in, core_in, plane, up, down, full, high, low, acc,
           sum_mine, sum_y, sum_core, sum_a, weight_sem,
           yp_s, yp_r, cp_s, cp_r, up_s, up_r, dn_s, dn_r, yq_s, yq_r, cq_s, cq_r,
           sy_s, sy_r, sc_s, sc_r, sa_s, sa_r):
    me = lax.axis_index("row")
    core = lax.rem(me, 2)
    b = lax.rem(me // 2, nb)
    a = me // (2 * nb)
    other = 1 - core
    units = chunks * panels * pieces
    width = pop.shape[4] // chunks
    block_rows, block_size = product.shape[0], product.shape[1]

    def at(a_, b_, core_):
        return {"row": (a_ * nb + b_) * 2 + core_}

    def b_plus(d):
        return lax.rem(b + d, nb)

    def b_minus(d):
        return lax.rem(b + nb - d, nb)

    def remote(src, dst, send, recv, where):
        return pltpu.make_async_remote_copy(
            src_ref=src, dst_ref=dst, send_sem=send, recv_sem=recv,
            device_id=where, device_id_type=MESH)

    load_weights = pltpu.make_async_copy(rates, weight_f32, weight_sem)
    load_weights.start()

    barrier = pltpu.get_barrier_semaphore()
    pl.semaphore_signal(barrier, inc=1, device_id=at(a, b, other), device_id_type=MESH)
    for d in range(1, nb):
        pl.semaphore_signal(barrier, inc=1, device_id=at(a, b_plus(d), core), device_id_type=MESH)
    for d in range(1, na):
        pl.semaphore_signal(barrier, inc=1, device_id=at(lax.rem(a + d, na), b, core),
                            device_id_type=MESH)
    pl.semaphore_wait(barrier, 1 + (nb - 1) + (na - 1))

    def y_pre(c, d):
        return remote(pop.at[:, b_plus(d), :, :, pl.ds(c * width, width)], y_in.at[c, d - 1],
                      yp_s.at[c, d - 1], yp_r.at[c, d - 1], at(a, b_plus(d), core))

    def core_pre(c, e):
        if e == 0:
            src = pop.at[other, b, :, :, pl.ds(c * width, width)]
        else:
            src = y_in.at[c, e - 1, other]
        return remote(src, core_in.at[c, e], cp_s.at[c, e], cp_r.at[c, e], at(a, b, other))

    def start_y(c):
        for d in range(1, nb):
            y_pre(c, d).start()

    def turn(c):
        for d in range(1, nb):
            y_pre(c, d).wait_recv()
        for e in range(nb):
            core_pre(c, e).start()

    def assemble(c):
        for e in range(nb):
            core_pre(c, e).wait_recv()
        plane[c, b * 2 + core] = pop[core, b, :, :, c * width:(c + 1) * width]
        plane[c, b * 2 + other] = core_in[c, 0]
        for d in range(1, nb):
            plane[c, b_minus(d) * 2 + core] = y_in[c, d - 1, core]
            plane[c, b_minus(d) * 2 + other] = core_in[c, d]

    start_y(0)
    acc[...] = jnp.zeros_like(acc)
    turn(0)
    for c in range(1, chunks):
        start_y(c)
    assemble(0)
    load_weights.wait()

    def up_copy(u):
        return remote(up.at[u], up.at[u], up_s.at[u], up_r.at[u], at(a + 1, b, core))

    def down_copy(u):
        return remote(down.at[u], down.at[u], dn_s.at[u], dn_r.at[u], at(a - 1, b, core))

    def y_post(u, d):
        here = full.at[u // pieces, core, b, lax.rem(u, pieces)]
        return remote(here, here, yq_s.at[u, d - 1], yq_r.at[u, d - 1], at(a, b_plus(d), core))

    def y_landed(u, d):
        here = full.at[u // pieces, core, b_minus(d), lax.rem(u, pieces)]
        return remote(here, here, yq_s.at[u, d - 1], yq_r.at[u, d - 1], at(a, b_minus(d), core))

    def core_copy(u, side):
        here = full.at[u // pieces, side, :, lax.rem(u, pieces)]
        return remote(here, here, cq_s.at[u], cq_r.at[u], at(a, b, other))

    def core_post(u):
        return core_copy(u, core)

    def core_landed(u):
        return core_copy(u, other)

    def panel_of(u):
        return lax.rem(u // pieces, panels)

    def flow(u, buffer, copy, first, last):
        owner = owners[panel_of(u)]

        def picked():
            return plane[u // (panels * pieces), lax.rem(owner, 2 * nb), lax.rem(u, pieces)]

        @pl.when(first)
        def _():
            buffer[u] = picked()

        @pl.when(jnp.logical_not(first))
        def _():
            copy(u).wait_recv()
            buffer[u] = jnp.where(owner // (2 * nb) == a, picked(), buffer[u])

        @pl.when(jnp.logical_not(last))
        def _():
            if THROTTLE:
                @pl.when(u >= THROTTLE)
                def _():
                    copy(u - THROTTLE).wait_send()
            copy(u).start()

    def prepare(k):
        def body(r, carry):
            for s in range(2):
                live = (s < counts[r, k]).astype(jnp.float32)
                hi, lo = split(weight_f32[r, k, s] * live)
                weights[k, r, 0:block_size, s * block_size:(s + 1) * block_size] = hi
                weights[k, r, block_size:2 * block_size,
                        s * block_size:(s + 1) * block_size] = lo
            return carry

        lax.fori_loop(0, block_rows, body, 0)

    def multiply(m):
        k = lax.rem(m, panels)
        c = m // panels

        @pl.when(m < panels)
        def _():
            prepare(k)

        hi, lo = split(full[m].reshape(block_rows, block_size, width))
        high[...] = hi
        low[...] = lo

        def body(r, carry):
            first, second = columns[r, k, 0], columns[r, k, 1]
            w = weights[k, r]
            p_hi = jnp.concatenate([high[first], high[second]], axis=0)
            p_lo = jnp.concatenate([low[first], low[second]], axis=0)
            both = jnp.dot(w, p_hi, preferred_element_type=jnp.float32)
            cross = jnp.dot(w[0:block_size], p_lo, preferred_element_type=jnp.float32)
            acc[c, r] += both[0:block_size] + (both[block_size:2 * block_size] + cross)
            return carry

        lax.fori_loop(0, block_rows, body, 0, unroll=True)

    def step(t, carry):
        for c in range(1, chunks):
            @pl.when(t == max((c * panels - 4) * pieces, 0))
            def _():
                turn(c)

            @pl.when(t == max((c * panels - 2) * pieces, 0))
            def _():
                assemble(c)

        lag_up, lag_down = SKEW * a, SKEW * (na - 1 - a)
        u_up, u_down = t - lag_up, t - lag_down
        u_y = t - jnp.maximum(lag_up, lag_down)
        u_c = u_y - LAG_Y
        u_m = u_c - LAG_C

        @pl.when((u_up >= 0) & (u_up < units))
        def _():
            flow(u_up, up, up_copy, a == 0, a == na - 1)

        @pl.when((u_down >= 0) & (u_down < units))
        def _():
            flow(u_down, down, down_copy, a == na - 1, a == 0)

        @pl.when((u_y >= 0) & (u_y < units))
        def _():
            owner_a = owners[panel_of(u_y)] // (2 * nb)
            full[u_y // pieces, core, b, lax.rem(u_y, pieces)] = jnp.where(owner_a <= a, up[u_y], down[u_y])
            for d in range(1, nb):
                y_post(u_y, d).start()

        @pl.when((u_c >= 0) & (u_c < units))
        def _():
            for d in range(1, nb):
                y_landed(u_c, d).wait_recv()
            core_post(u_c).start()

        @pl.when((u_m >= 0) & (u_m < units))
        def _():
            core_landed(u_m).wait_recv()

            @pl.when(lax.rem(u_m, pieces) == pieces - 1)
            def _():
                multiply(u_m // pieces)

        return carry

    lax.fori_loop(0, units + SKEW * (na - 1) + LAG_Y + LAG_C, step, 0)

    for c in range(chunks):
        x = acc[c].reshape(block_rows * block_size // 8, 8, width)
        sum_mine[0, :, c * width:(c + 1) * width] = jnp.sum(x * x, axis=0)

    def sum_c():
        return remote(sum_mine.at[0], sum_core, sc_s, sc_r, at(a, b, other))

    def sum_b(d):
        return remote(sum_mine.at[1], sum_y.at[d - 1], sy_s.at[d - 1], sy_r.at[d - 1],
                      at(a, b_plus(d), core))

    def sum_over_a(d):
        return remote(sum_mine.at[2], sum_a.at[d - 1], sa_s.at[d - 1], sa_r.at[d - 1],
                      at(lax.rem(a + d, na), b, core))

    sum_c().start()
    for c in range(chunks):
        product[:, :, c * width:(c + 1) * width] = acc[c]
    sum_c().wait_recv()
    sum_mine[1] = sum_mine[0] + sum_core[...]
    for d in range(1, nb):
        sum_b(d).start()
    total = sum_mine[1]
    for d in range(1, nb):
        sum_b(d).wait_recv()
        total = total + sum_y[d - 1]
    sum_mine[2] = total
    for d in range(1, na):
        sum_over_a(d).start()
    for d in range(1, na):
        sum_over_a(d).wait_recv()
        total = total + sum_a[d - 1]
    squares[...] = total

    sum_c().wait_send()
    for d in range(1, nb):
        sum_b(d).wait_send()
    for d in range(1, na):
        sum_over_a(d).wait_send()
    for c in range(chunks):
        for d in range(1, nb):
            y_pre(c, d).wait_send()
        for e in range(nb):
            core_pre(c, e).wait_send()

    def drain(u, carry):
        left = u >= units - THROTTLE if THROTTLE else True

        @pl.when((a < na - 1) & left)
        def _():
            up_copy(u).wait_send()

        @pl.when((a > 0) & left)
        def _():
            down_copy(u).wait_send()

        for d in range(1, nb):
            y_post(u, d).wait_send()
        core_post(u).wait_send()
        return carry

    lax.fori_loop(0, units, drain, 0)


def on_device(devices, populations, rate_blocks, columns, counts, owners):
    block_rows, panels, slots, block_size, _ = rate_blocks.shape
    rows, chains = populations.shape
    na, nb = grid_of(devices)
    chunks = CHUNKS
    pieces = PIECES
    units = chunks * panels * pieces
    width = chains // chunks
    piece_rows = rows // (2 * nb * pieces)
    f32, bf16 = jnp.float32, jnp.bfloat16
    vmem = pl.BlockSpec(memory_space=pltpu.VMEM)
    smem = pl.BlockSpec(memory_space=pltpu.SMEM)
    dma = pltpu.SemaphoreType.DMA
    product, squares = pl.pallas_call(
        functools.partial(kernel, na, nb, chunks, pieces, panels),
        out_shape=(jax.ShapeDtypeStruct((block_rows, block_size, chains), f32),
                   jax.ShapeDtypeStruct((8, chains), f32)),
        in_specs=[vmem, pl.BlockSpec(memory_space=pl.ANY), smem, smem, smem],
        out_specs=(vmem, vmem),
        scratch_shapes=[
            pltpu.VMEM((block_rows, panels, slots, block_size, block_size), f32),
            pltpu.VMEM((panels, block_rows, 2 * block_size, slots * block_size), bf16),
            pltpu.VMEM((chunks, nb - 1, 2, pieces, piece_rows, width), f32),
            pltpu.VMEM((chunks, nb, pieces, piece_rows, width), f32),
            pltpu.VMEM((chunks, 2 * nb, pieces, piece_rows, width), f32),
            pltpu.VMEM((units, piece_rows, width), f32),
            pltpu.VMEM((units, piece_rows, width), f32),
            pltpu.VMEM((chunks * panels, 2, nb, pieces, piece_rows, width), f32),
            pltpu.VMEM((block_rows, block_size, width), bf16),
            pltpu.VMEM((block_rows, block_size, width), bf16),
            pltpu.VMEM((chunks, block_rows, block_size, width), f32),
            pltpu.VMEM((3, 8, chains), f32),
            pltpu.VMEM((nb - 1, 8, chains), f32),
            pltpu.VMEM((8, chains), f32),
            pltpu.VMEM((na - 1, 8, chains), f32),
            dma,
            dma((chunks, nb - 1)), dma((chunks, nb - 1)),
            dma((chunks, nb)), dma((chunks, nb)),
            dma((units,)), dma((units,)),
            dma((units,)), dma((units,)),
            dma((units, nb - 1)), dma((units, nb - 1)),
            dma((units,)), dma((units,)),
            dma((nb - 1,)), dma((nb - 1,)),
            dma, dma,
            dma((na - 1,)), dma((na - 1,)),
        ],
        compiler_params=pltpu.CompilerParams(
            collective_id=0, has_side_effects=True, vmem_limit_bytes=56 * 1024 * 1024),
        cost_estimate=pl.CostEstimate(
            flops=6 * block_rows * panels * slots * block_size * block_size * chains,
            bytes_accessed=4 * (rate_blocks.size + 2 * populations.size), transcendentals=0),
    )(populations.reshape(2, nb, pieces, piece_rows, chains), rate_blocks, columns, counts, owners)
    chain_scale = jnp.sqrt(jnp.sum(squares, axis=0) / (rows * devices) + 1e-06)
    return product.reshape(rows, chains) / chain_scale, chain_scale


def solution(mesh):
    in_specs = (
        P(("grp", "row"), None),
        P(("grp", "row"), None, None, None, None),
        P(("grp", "row"), None, None),
        P(("grp", "row"), None),
        P(),
    )
    out_specs = (P(("grp", "row"), None), P("grp"))
    return jax.shard_map(
        functools.partial(on_device, mesh.shape["row"]),
        mesh=mesh, in_specs=in_specs, out_specs=out_specs, check_vma=False)
```
